128 devices in a mesh: blk: 32 (over z, x_hi, y), layer: 4 (over x_lo, core).
Axes of the slice: x: 4 (x_hi: 2, x_lo: 2; x = x_hi * 2 + x_lo), y: 4, z: 4, core: 2. Of those that a mesh axis runs over, the one named last changes fastest.
Arguments:
- density: float32 [32768, 3, 1024], P('blk', None, 'layer'), may hold values from -0.80592746 to 0.80592746
- tile_mask: int32 [256, 3, 8], P('blk', None, 'layer'), may hold values 0 or 1
Outputs:
- squared: float32 [32768, 5, 1024], P('blk', None, 'layer')
The draws below stay inside these ranges and needn't reach their ends.
All inputs are finite; a program needn't handle non-finite values. No bound on the sum of `tile_mask` on one device may be relied on, other than what follows from the above.
Results may differ from the reference program's by a relative error of at most 0.0003.
Values sent between devices are 32-bit elements; how exact they have to be, the bound alone decides.
A program may use at most 128 MiB of HBM per device.

```python
import jax
import jax.numpy as jnp
from jax import lax

TILE = 128
RT = 8
W = 1024
NB = 32
M = 32768


def touch_ends(drawn, stream_key, smallest, top_value):
    longest = drawn.shape.index(max(drawn.shape))
    spots = []
    for shift in (0, 1):
        where = [jax.random.randint(jax.random.fold_in(stream_key, axis), (), 0, length) for axis, length in enumerate(drawn.shape)]
        where[longest] = (where[longest] + shift) % drawn.shape[longest]
        spots.append(tuple(where))
    return drawn.at[spots[0]].set(smallest).at[spots[1]].set(top_value)


def block_levels(rng, dims, cuts, low, high):
    def one(dim, parts):
        draws = jax.random.uniform(jax.random.fold_in(jax.random.fold_in(rng, 6), dim), (parts,), jnp.float32, low / len(cuts), high / len(cuts))
        return jnp.repeat(jnp.exp(draws), dims[dim] // parts).reshape((-1,) + (1,) * (len(dims) - dim - 1))

    factor_of = one(*cuts[0])
    for cut in cuts[1:]:
        factor_of = factor_of * one(*cut)
    return factor_of


def scatter_about(own_key, dims, spread, most, pieces=(), held_as=jnp.bfloat16):
    gain = block_levels(own_key, dims, pieces, -0.22, 0.18) if pieces else 1.0
    drawn = jax.random.normal(own_key, dims, jnp.float32) * spread * gain
    return jnp.minimum(jnp.maximum(drawn, -most), most).astype(held_as)


def setup_inputs(seed: int = 0) -> dict:
    splits = jax.random.split(jax.random.key(seed), 3)
    density = scatter_about(splits[0], (M, 3, W), ((3 * RT * TILE) ** -0.25), 0.80592746, ((0, 32), (2, 4)), jnp.float32)
    tile_mask = touch_ends((jax.random.randint(splits[1], (M // TILE, 3, W // TILE), 0, 4) < 3).astype(jnp.int32), jax.random.fold_in(splits[1], 1), 0, 1)
    return {"density": density, "tile_mask": tile_mask}


def reference(density, tile_mask):
    expanded = jnp.repeat(jnp.repeat(tile_mask, TILE, axis=0), TILE, axis=2).astype(jnp.float32)
    kept = (density * expanded).reshape(NB, W, 3, W)

    def one_block(index):
        result = jnp.zeros((W, 5, W), jnp.float32)
        for offset in range(3):
            other = kept[(index + offset - 1) % NB].reshape(W, 3 * W)
            left = kept[index][:, offset, :]
            term = jnp.dot(left, other, preferred_element_type=jnp.float32, precision=lax.Precision.HIGHEST)
            result = result.at[:, offset:offset + 3, :].add(term.reshape(W, 3, W))
        return result

    blocks = lax.map(one_block, jnp.arange(NB, dtype=jnp.int32))
    return blocks.reshape(NB * W, 5, W)
```

```python
import functools

import jax
import jax.numpy as jnp
from jax import lax
from jax.experimental import pallas as pl
from jax.experimental.pallas import tpu as pltpu
from jax.sharding import PartitionSpec as P

TILE = 128
Q = 256
SUB = 64
NSUB = Q // SUB
Y = 4
F32 = jnp.float32
BF16 = jnp.bfloat16
MESH = pl.DeviceIdType.MESH
BLOCKS = [(rho, b) for rho in range(4) for b in range(3)]


def kernel(
    dens, mask, out, own, sib, par, fwd, pre, fol, lh, ll, rh, rl,
    load_sem, sib_send, sib_recv, par_send, par_recv, fwd_send, fwd_recv,
    nxt_send, pre_recv, prv_send, fol_recv,
):
    blk = lax.axis_index("blk")
    lay = lax.axis_index("layer")
    nblk = lax.axis_size("blk")
    half = lay // 2
    core = lay % 2
    y = lax.rem(blk, Y)
    at_end = y == Y - 1
    at_start = y == 0
    other_half = (1 - half) * 2 + core
    partner = (blk, other_half)
    sibling = (blk, half * 2 + 1 - core)
    nxt = (lax.rem(blk + 1, nblk), jnp.where(at_end, other_half, lay))
    prv = (lax.rem(blk + nblk - 1, nblk), jnp.where(at_start, other_half, lay))

    def row_of(rho):
        return pl.multiple_of(lax.rem(2 * half + rho, 4) * Q, Q)

    def par_row_of(rho):
        return pl.multiple_of(lax.rem(2 * half + 2 + rho, 4) * Q, Q)

    def remote(src, dst, send, recv, to):
        return pltpu.make_async_remote_copy(
            src_ref=src, dst_ref=dst, send_sem=send, recv_sem=recv,
            device_id=to, device_id_type=MESH,
        )

    def load(k, rho, b):
        rows = pl.ds(row_of(rho), Q)
        return pltpu.make_async_copy(dens.at[b, rows], own.at[b, rows], load_sem.at[k])

    def to_sibling(k, rho, b):
        rows = pl.ds(row_of(rho), Q)
        return remote(own.at[b, rows], sib.at[b, rows], sib_send.at[k], sib_recv.at[k], sibling)

    def to_partner(k, rho, b, s):
        rows = pl.ds(row_of(rho) + s * SUB, SUB)
        return remote(own.at[b, rows], par.at[b, rows], par_send.at[k], par_recv.at[k, s], partner)

    def block_to_next(k, rho, b):
        rows = pl.ds(row_of(rho), Q)
        return remote(own.at[b, rows], pre.at[b, rows], nxt_send.at[k], pre_recv.at[k], nxt)

    def block_to_prev(k, rho, b):
        rows = pl.ds(row_of(rho), Q)
        return remote(own.at[b, rows], fol.at[b, rows], prv_send.at[k], fol_recv.at[k], prv)

    def send_block(k):
        rho, b = BLOCKS[k]
        for s in range(NSUB):
            to_partner(k, rho, b, s).start()

        @pl.when(jnp.logical_not(at_end))
        def _():
            block_to_next(k, rho, b).start()

        @pl.when(jnp.logical_not(at_start))
        def _():
            block_to_prev(k, rho, b).start()

    def forward(k, s):
        rho, b = BLOCKS[k]
        rows = pl.ds(par_row_of(rho) + s * SUB, SUB)
        remote(own.at[b, rows], par.at[b, rows], par_send.at[k], par_recv.at[k, s], partner).wait_recv()
        remote(par.at[b, rows], fwd.at[b, rows], fwd_send.at[k], fwd_recv.at[k], sibling).start()

        @pl.when(at_end)
        def _():
            remote(par.at[b, rows], pre.at[b, rows], nxt_send.at[k], pre_recv.at[k], nxt).start()

        @pl.when(at_start)
        def _():
            remote(par.at[b, rows], fol.at[b, rows], prv_send.at[k], fol_recv.at[k], prv).start()

    def split(x):
        hi = x.astype(BF16)
        return hi, (x - hi.astype(F32)).astype(BF16)

    def keep_left(slot, o, r0, n, x):
        hi, lo = split(x)
        lh[slot, o, pl.ds(r0, n), :] = hi
        ll[slot, o, pl.ds(r0, n), :] = lo

    def mask_own(rho, b):
        r0 = row_of(rho)
        t0 = lax.rem(2 * half + rho, 4) * 2
        for t in range(2):
            for j in range(2):
                m = mask[b, j, t0 + t].astype(F32)
                rows = pl.ds(r0 + t * TILE, TILE)
                cols = pl.ds(j * TILE, TILE)
                x = own[b, rows, cols] * m
                own[b, rows, cols] = x
                hi, lo = split(x)
                lh[core, b, rows, cols] = hi
                ll[core, b, rows, cols] = lo

    def product(o, b, rho, r0, n):
        rows = pl.ds(r0, n)
        ah = lh[rho, o, rows, :]
        al = ll[rho, o, rows, :]
        if o == 1:
            inner = pl.ds(row_of(rho), Q)
            wh = lh[core, b, inner, :]
            wl = ll[core, b, inner, :]
        else:
            wh = rh[o // 2, rho, b]
            wl = rl[o // 2, rho, b]
        dot = functools.partial(jnp.dot, preferred_element_type=F32)
        out[o + b, rows, :] += dot(ah, wh) + dot(ah, wl) + dot(al, wh)

    def arrive(k):
        rho, b = BLOCKS[k]
        prow = par_row_of(rho)
        rows = pl.ds(prow, Q)
        keep_left(2 + core, b, prow, Q, par[b, rows, :])
        remote(par.at[b, rows], fwd.at[b, rows], fwd_send.at[k], fwd_recv.at[k], sibling).wait_recv()
        keep_left(3 - core, b, prow, Q, fwd[b, rows, :])
        krows = pl.ds(row_of(rho), Q)
        block_to_next(k, rho, b).wait_recv()
        hi, lo = split(pre[b, krows, :])
        rh[0, rho, b] = hi
        rl[0, rho, b] = lo
        block_to_prev(k, rho, b).wait_recv()
        hi, lo = split(fol[b, krows, :])
        rh[1, rho, b] = hi
        rl[1, rho, b] = lo

    first = pl.multiple_of((1 - half) * 2 * Q, 2 * Q)

    def work(k):
        rho, b = BLOCKS[k]
        third, fourth = par_row_of(2), par_row_of(3)
        todo = [functools.partial(arrive, k)]

        def add(*what):
            todo.append(functools.partial(product, *what))

        if rho < 2:
            for o in (0, 2):
                add(o, b, rho, 0, 4 * Q)
        else:
            for o in (0, 2):
                have = 3 * (rho - 2) + b - o
                if have >= 3:
                    add(o, b, rho, 0, 4 * Q)
                else:
                    add(o, b, rho, first, 2 * Q)
                    if have >= 0:
                        add(o, b, rho, third, Q)
            if b != 1:
                rows = third if rho == 2 else fourth
                for r in (2, 3):
                    for c in range(3):
                        if 3 * r + c < k:
                            add(b, c, r, rows, Q)
        if b == 1:
            for c in range(3):
                for r in (2, 3):
                    add(1, c, r, par_row_of(rho), Q)
        return todo

    for k, (rho, b) in enumerate(BLOCKS):
        load(k, rho, b).start()
    barrier = pltpu.get_barrier_semaphore()
    for device in (partner, sibling, nxt, prv):
        pl.semaphore_signal(barrier, inc=1, device_id=device, device_id_type=MESH)
    for k in range(2):
        load(k, *BLOCKS[k]).wait()
        mask_own(*BLOCKS[k])
    pl.semaphore_wait(barrier, 4)
    for k in range(2):
        send_block(k)
        to_sibling(k, *BLOCKS[k]).start()
    for k in range(2, 12):
        load(k, *BLOCKS[k]).wait()
        mask_own(*BLOCKS[k])
        to_sibling(k, *BLOCKS[k]).start()
    for j in range(5):
        out[j] = jnp.zeros_like(out[j])

    def sib_block(k):
        rho, b = BLOCKS[k]
        to_sibling(k, rho, b).wait_recv()
        rows = pl.ds(row_of(rho), Q)
        keep_left(1 - core, b, row_of(rho), Q, sib[b, rows, :])

    queue = [(0, functools.partial(sib_block, k)) for k in range(12)]
    queue += [(0, functools.partial(product, 1, b, r, 0, 4 * Q)) for b in range(3) for r in range(2)]
    for k in range(12):
        queue += [(min(NSUB * (k + 1) + 1, 12 * NSUB - 1) if k < 11 else 12 * NSUB, t) for t in work(k)]
    at = 0
    for s in range(12 * NSUB):
        k, piece = divmod(s, NSUB)
        if piece == 0 and k + 2 < 12:
            send_block(k + 2)
        forward(k, piece)
        done = 0
        limit = 4 if s < 12 * NSUB - 4 else 3
        while at < len(queue) and queue[at][0] <= s and done < limit:
            queue[at][1]()
            at += 1
            done += 1
    for _, thunk in queue[at:]:
        thunk()

    for k, (rho, b) in enumerate(BLOCKS):
        rows = pl.ds(row_of(rho), Q)
        prow = pl.ds(par_row_of(rho), Q)
        to_sibling(k, rho, b).wait_send()
        remote(own.at[b, rows], par.at[b, rows], par_send.at[k], par_recv.at[k, 0], partner).wait_send()
        remote(par.at[b, prow], fwd.at[b, prow], fwd_send.at[k], fwd_recv.at[k], sibling).wait_send()
        block_to_next(k, rho, b).wait_send()
        block_to_prev(k, rho, b).wait_send()


def local(density, tile_mask):
    dens = jnp.transpose(density, (1, 0, 2))
    mask = jnp.transpose(tile_mask, (1, 2, 0))
    panel = pltpu.VMEM(dens.shape, F32)
    dma = pltpu.SemaphoreType.DMA
    rows, cols = dens.shape[1:]
    out = pl.pallas_call(
        kernel,
        out_shape=jax.ShapeDtypeStruct((5, rows, cols), F32),
        in_specs=[pl.BlockSpec(memory_space=pl.ANY), pl.BlockSpec(memory_space=pltpu.SMEM)],
        out_specs=pl.BlockSpec(memory_space=pltpu.VMEM),
        scratch_shapes=[panel] * 6
        + [pltpu.VMEM((4, 3, rows, cols), BF16)] * 2
        + [pltpu.VMEM((2, 4, 3, Q, cols), BF16)] * 2
        + [dma((12,))] * 4
        + [dma((12, NSUB))]
        + [dma((12,))] * 6,
        compiler_params=pltpu.CompilerParams(
            collective_id=0, has_side_effects=True, vmem_limit_bytes=60 * 1024 * 1024
        ),
    )(dens, mask)
    return jnp.transpose(out, (1, 0, 2))


def solution(mesh):
    placed = (P("blk", None, "layer"), P("blk", None, "layer"))
    return jax.shard_map(
        local, mesh=mesh, in_specs=placed, out_specs=P("blk", None, "layer"), check_vma=False
    )
```

```python
import functools

import jax
import jax.numpy as jnp
from jax import lax
from jax.experimental import pallas as pl
from jax.experimental.pallas import tpu as pltpu
from jax.sharding import PartitionSpec as P

TILE = 128
Q = 256
PIECES = [[32, 32, 64, 64, 64]] + [[64] * 4] * 10 + [[64, 64, 64, 32, 32]]
STEPS = [(k, sum(rows[:i]), n, i) for k, rows in enumerate(PIECES) for i, n in enumerate(rows)]
LAST = [max(s for s, step in enumerate(STEPS) if step[0] == k) for k in range(12)]
LEFT_LAG, RIGHT_LAG = 2, 7
BUDGET = 128 * 5
Y = 4
F32 = jnp.float32
BF16 = jnp.bfloat16
MESH = pl.DeviceIdType.MESH
BLOCKS = [(rho, b) for rho in range(4) for b in range(3)]


def kernel(
    dens, mask, out, own, sib, par, fwd, pre, fol, lh, ll, rh, rl,
    load_sem, sib_send, sib_recv, par_send, par_recv, fwd_send, fwd_recv,
    nxt_send, pre_recv, prv_send, fol_recv,
):
    blk = lax.axis_index("blk")
    lay = lax.axis_index("layer")
    nblk = lax.axis_size("blk")
    half = lay // 2
    core = lay % 2
    y = lax.rem(blk, Y)
    at_end = y == Y - 1
    at_start = y == 0
    other_half = (1 - half) * 2 + core
    partner = (blk, other_half)
    sibling = (blk, half * 2 + 1 - core)
    nxt = (lax.rem(blk + 1, nblk), jnp.where(at_end, other_half, lay))
    prv = (lax.rem(blk + nblk - 1, nblk), jnp.where(at_start, other_half, lay))

    def row_of(rho):
        return pl.multiple_of(lax.rem(2 * half + rho, 4) * Q, Q)

    def par_row_of(rho):
        return pl.multiple_of(lax.rem(2 * half + 2 + rho, 4) * Q, Q)

    def remote(src, dst, send, recv, to):
        return pltpu.make_async_remote_copy(
            src_ref=src, dst_ref=dst, send_sem=send, recv_sem=recv,
            device_id=to, device_id_type=MESH,
        )

    def load(k, rho, b):
        rows = pl.ds(row_of(rho), Q)
        return pltpu.make_async_copy(dens.at[b, rows], own.at[b, rows], load_sem.at[k])

    def to_sibling(k, rho, b):
        rows = pl.ds(row_of(rho), Q)
        return remote(own.at[b, rows], sib.at[b, rows], sib_send.at[k], sib_recv.at[k], sibling)

    def to_partner(k, offset, n, i):
        rho, b = BLOCKS[k]
        rows = pl.ds(row_of(rho) + offset, n)
        return remote(own.at[b, rows], par.at[b, rows], par_send.at[k], par_recv.at[k, i], partner)

    def block_to_next(k, rho, b):
        rows = pl.ds(row_of(rho), Q)
        return remote(own.at[b, rows], pre.at[b, rows], nxt_send.at[k], pre_recv.at[k], nxt)

    def block_to_prev(k, rho, b):
        rows = pl.ds(row_of(rho), Q)
        return remote(own.at[b, rows], fol.at[b, rows], prv_send.at[k], fol_recv.at[k], prv)

    def send_block(k):
        rho, b = BLOCKS[k]
        for step in STEPS:
            if step[0] == k:
                to_partner(*step).start()

        @pl.when(jnp.logical_not(at_end))
        def _():
            block_to_next(k, rho, b).start()

        @pl.when(jnp.logical_not(at_start))
        def _():
            block_to_prev(k, rho, b).start()

    def forward(k, offset, n, i):
        rho, b = BLOCKS[k]
        rows = pl.ds(par_row_of(rho) + offset, n)
        remote(own.at[b, rows], par.at[b, rows], par_send.at[k], par_recv.at[k, i], partner).wait_recv()
        remote(par.at[b, rows], fwd.at[b, rows], fwd_send.at[k], fwd_recv.at[k], sibling).start()

        @pl.when(at_end)
        def _():
            remote(par.at[b, rows], pre.at[b, rows], nxt_send.at[k], pre_recv.at[k], nxt).start()

        @pl.when(at_start)
        def _():
            remote(par.at[b, rows], fol.at[b, rows], prv_send.at[k], fol_recv.at[k], prv).start()

    def split(x):
        hi = x.astype(BF16)
        return hi, (x - hi.astype(F32)).astype(BF16)

    def keep_left(slot, o, r0, n, x):
        hi, lo = split(x)
        lh[slot, o, pl.ds(r0, n), :] = hi
        ll[slot, o, pl.ds(r0, n), :] = lo

    def mask_own(rho, b):
        r0 = row_of(rho)
        t0 = lax.rem(2 * half + rho, 4) * 2
        for t in range(2):
            for j in range(2):
                m = mask[b, j, t0 + t].astype(F32)
                rows = pl.ds(r0 + t * TILE, TILE)
                cols = pl.ds(j * TILE, TILE)
                x = own[b, rows, cols] * m
                own[b, rows, cols] = x
                hi, lo = split(x)
                lh[core, b, rows, cols] = hi
                ll[core, b, rows, cols] = lo

    def product(o, b, rho, r0, n):
        rows = pl.ds(r0, n)
        ah = lh[rho, o, rows, :]
        al = ll[rho, o, rows, :]
        if o == 1:
            inner = pl.ds(row_of(rho), Q)
            wh = lh[core, b, inner, :]
            wl = ll[core, b, inner, :]
        else:
            wh = rh[o // 2, rho, b]
            wl = rl[o // 2, rho, b]
        dot = functools.partial(jnp.dot, preferred_element_type=F32)
        out[o + b, rows, :] += dot(ah, wh) + dot(ah, wl) + dot(al, wh)

    def left_arrives(k):
        rho, b = BLOCKS[k]
        prow = par_row_of(rho)
        rows = pl.ds(prow, Q)
        keep_left(2 + core, b, prow, Q, par[b, rows, :])
        remote(par.at[b, rows], fwd.at[b, rows], fwd_send.at[k], fwd_recv.at[k], sibling).wait_recv()
        keep_left(3 - core, b, prow, Q, fwd[b, rows, :])

    def right_arrives(k):
        rho, b = BLOCKS[k]
        rows = pl.ds(row_of(rho), Q)
        block_to_next(k, rho, b).wait_recv()
        hi, lo = split(pre[b, rows, :])
        rh[0, rho, b] = hi
        rl[0, rho, b] = lo
        block_to_prev(k, rho, b).wait_recv()
        hi, lo = split(fol[b, rows, :])
        rh[1, rho, b] = hi
        rl[1, rho, b] = lo

    def sibling_arrives(k):
        rho, b = BLOCKS[k]
        to_sibling(k, rho, b).wait_recv()
        r0 = row_of(rho)
        keep_left(1 - core, b, r0, Q, sib[b, pl.ds(r0, Q), :])

    first = pl.multiple_of((1 - half) * 2 * Q, 2 * Q)
    queue = []

    def add(when, cost, what, *args):
        queue.append((min(when, len(STEPS)), cost, functools.partial(what, *args)))

    def add_product(when, *args):
        add(when, args[-1], product, *args)

    for k in range(12):
        add(0, Q, sibling_arrives, k)
    for b in range(3):
        for rho in range(2):
            add_product(0, 1, b, rho, 0, 4 * Q)
    for k, (rho, b) in enumerate(BLOCKS):
        with_left = LAST[k] + LEFT_LAG
        with_right = LAST[k] + RIGHT_LAG
        crossed = LAST[k - 1] + RIGHT_LAG if k else 0
        rows = par_row_of(rho)
        add(with_left, 2 * Q, left_arrives, k)
        if b == 1:
            for c in range(3):
                for r in (2, 3):
                    add_product(with_left, 1, c, r, rows, Q)
        elif rho >= 2:
            for r in (2, 3):
                for c in range(3):
                    if 3 * r + c < k:
                        add_product(max(with_left, crossed), b, c, r, rows, Q)
        add(with_right, 2 * Q, right_arrives, k)
        for o in (0, 2):
            if rho < 2 or 3 * rho + b >= 9 + o:
                add_product(with_right, o, b, rho, 0, 4 * Q)
            else:
                add_product(with_right, o, b, rho, first, 2 * Q)
                if 3 * rho + b >= 6 + o:
                    add_product(with_right, o, b, rho, par_row_of(2), Q)
    queue.sort(key=lambda entry: entry[0])

    for k, (rho, b) in enumerate(BLOCKS):
        load(k, rho, b).start()
    barrier = pltpu.get_barrier_semaphore()
    for device in (partner, sibling, nxt, prv):
        pl.semaphore_signal(barrier, inc=1, device_id=device, device_id_type=MESH)
    for k in range(2):
        load(k, *BLOCKS[k]).wait()
        mask_own(*BLOCKS[k])
    pl.semaphore_wait(barrier, 4)
    for k in range(2):
        send_block(k)
        to_sibling(k, *BLOCKS[k]).start()
    for k in range(2, 12):
        load(k, *BLOCKS[k]).wait()
        mask_own(*BLOCKS[k])
        to_sibling(k, *BLOCKS[k]).start()
    for j in range(5):
        out[j] = jnp.zeros_like(out[j])

    for s, step in enumerate(STEPS):
        k, _, _, i = step
        if i == 0 and k + 2 < 12:
            send_block(k + 2)
        forward(*step)
        spent = 0
        while queue and queue[0][0] <= s and spent < BUDGET:
            _, cost, what = queue.pop(0)
            what()
            spent += cost
    for _, _, what in queue:
        what()

    for k, (rho, b) in enumerate(BLOCKS):
        rows = pl.ds(row_of(rho), Q)
        prow = pl.ds(par_row_of(rho), Q)
        to_sibling(k, rho, b).wait_send()
        remote(own.at[b, rows], par.at[b, rows], par_send.at[k], par_recv.at[k, 0], partner).wait_send()
        remote(par.at[b, prow], fwd.at[b, prow], fwd_send.at[k], fwd_recv.at[k], sibling).wait_send()
        block_to_next(k, rho, b).wait_send()
        block_to_prev(k, rho, b).wait_send()


def local(density, tile_mask):
    dens = jnp.transpose(density, (1, 0, 2))
    mask = jnp.transpose(tile_mask, (1, 2, 0))
    panel = pltpu.VMEM(dens.shape, F32)
    dma = pltpu.SemaphoreType.DMA
    rows, cols = dens.shape[1:]
    out = pl.pallas_call(
        kernel,
        out_shape=pltpu.VMEM((5, rows, cols), F32),
        in_specs=[pl.BlockSpec(memory_space=pl.ANY), pl.BlockSpec(memory_space=pltpu.SMEM)],
        out_specs=pl.BlockSpec(memory_space=pltpu.VMEM),
        scratch_shapes=[panel] * 6
        + [pltpu.VMEM((4, 3, rows, cols), BF16)] * 2
        + [pltpu.VMEM((2, 4, 3, Q, cols), BF16)] * 2
        + [dma((12,))] * 4
        + [dma((12, max(map(len, PIECES))))]
        + [dma((12,))] * 6,
        compiler_params=pltpu.CompilerParams(
            collective_id=0, has_side_effects=True, vmem_limit_bytes=50 * 1024 * 1024
        ),
    )(dens, mask)
    return jnp.transpose(out, (1, 0, 2))


def solution(mesh):
    placed = (P("blk", None, "layer"), P("blk", None, "layer"))
    return jax.shard_map(
        local, mesh=mesh, in_specs=placed, out_specs=P("blk", None, "layer"), check_vma=False
    )
```

```python
import functools

import jax
import jax.numpy as jnp
from jax import lax
from jax.experimental import pallas as pl
from jax.experimental.pallas import tpu as pltpu
from jax.sharding import PartitionSpec as P

TILE = 128
Q = 256
PIECES = [[48, 48, 56, 56, 48]] * 12
STEPS = [(k, sum(rows[:i]), n, i) for k, rows in enumerate(PIECES) for i, n in enumerate(rows)]
LAST = [max(s for s, step in enumerate(STEPS) if step[0] == k) for k in range(12)]
LEFT_LAG, RIGHT_LAG = 2, 9
BUDGET = 128 * 5
Y = 4
F32 = jnp.float32
BF16 = jnp.bfloat16
MESH = pl.DeviceIdType.MESH
BLOCKS = [(rho, b) for rho in range(4) for b in range(3)]


def kernel(
    dens, mask, out, lh, ll, last_h, last_l, own, sib, par, fwd, pre, fol, rh, rl,
    load_sem, sib_send, sib_recv, par_send, par_recv, fwd_send, fwd_recv,
    nxt_send, pre_recv, prv_send, fol_recv,
):
    blk = lax.axis_index("blk")
    lay = lax.axis_index("layer")
    nblk = lax.axis_size("blk")
    half = lay // 2
    core = lay % 2
    y = lax.rem(blk, Y)
    at_end = y == Y - 1
    at_start = y == 0
    other_half = (1 - half) * 2 + core
    partner = (blk, other_half)
    sibling = (blk, half * 2 + 1 - core)
    nxt = (lax.rem(blk + 1, nblk), jnp.where(at_end, other_half, lay))
    prv = (lax.rem(blk + nblk - 1, nblk), jnp.where(at_start, other_half, lay))

    def row_of(rho):
        return pl.multiple_of(lax.rem(2 * half + rho, 4) * Q, Q)

    def par_row_of(rho):
        return pl.multiple_of(lax.rem(2 * half + 2 + rho, 4) * Q, Q)

    def remote(src, dst, send, recv, to):
        return pltpu.make_async_remote_copy(
            src_ref=src, dst_ref=dst, send_sem=send, recv_sem=recv,
            device_id=to, device_id_type=MESH,
        )

    def load(k, rho, b):
        rows = pl.ds(row_of(rho), Q)
        return pltpu.make_async_copy(dens.at[b, rows], own.at[b, rows], load_sem.at[k])

    def to_sibling(k, rho, b):
        rows = pl.ds(row_of(rho), Q)
        return remote(own.at[b, rows], sib.at[b, rows], sib_send.at[k], sib_recv.at[k], sibling)

    def to_partner(k, offset, n, i):
        rho, b = BLOCKS[k]
        rows = pl.ds(row_of(rho) + offset, n)
        return remote(own.at[b, rows], par.at[b, rows], par_send.at[k], par_recv.at[k, i], partner)

    def block_to_next(k, rho, b):
        rows = pl.ds(row_of(rho), Q)
        return remote(own.at[b, rows], pre.at[b, rows], nxt_send.at[k], pre_recv.at[k], nxt)

    def block_to_prev(k, rho, b):
        rows = pl.ds(row_of(rho), Q)
        return remote(own.at[b, rows], fol.at[b, rows], prv_send.at[k], fol_recv.at[k], prv)

    def send_block(k):
        rho, b = BLOCKS[k]
        for step in STEPS:
            if step[0] == k:
                to_partner(*step).start()

        @pl.when(jnp.logical_not(at_end))
        def _():
            block_to_next(k, rho, b).start()

        @pl.when(jnp.logical_not(at_start))
        def _():
            block_to_prev(k, rho, b).start()

    def forward(k, offset, n, i):
        rho, b = BLOCKS[k]
        rows = pl.ds(par_row_of(rho) + offset, n)
        remote(own.at[b, rows], par.at[b, rows], par_send.at[k], par_recv.at[k, i], partner).wait_recv()
        remote(par.at[b, rows], fwd.at[b, rows], fwd_send.at[k], fwd_recv.at[k], sibling).start()

        @pl.when(at_end)
        def _():
            remote(par.at[b, rows], pre.at[b, rows], nxt_send.at[k], pre_recv.at[k], nxt).start()

        @pl.when(at_start)
        def _():
            remote(par.at[b, rows], fol.at[b, rows], prv_send.at[k], fol_recv.at[k], prv).start()

    def split(x):
        hi = x.astype(BF16)
        return hi, (x - hi.astype(F32)).astype(BF16)

    def keep_left(slot, o, r0, n, x):
        hi, lo = split(x)
        lh[slot, o, pl.ds(r0, n), :] = hi
        ll[slot, o, pl.ds(r0, n), :] = lo

    def mask_own(rho, b):
        r0 = row_of(rho)
        t0 = lax.rem(2 * half + rho, 4) * 2
        for t in range(2):
            for j in range(2):
                m = mask[b, j, t0 + t].astype(F32)
                rows = pl.ds(r0 + t * TILE, TILE)
                cols = pl.ds(j * TILE, TILE)
                x = own[b, rows, cols] * m
                own[b, rows, cols] = x
                hi, lo = split(x)
                lh[core, b, rows, cols] = hi
                ll[core, b, rows, cols] = lo

    def product(o, b, rho, r0, n):
        rows = pl.ds(r0, n)
        ah = lh[rho, o, rows, :]
        al = ll[rho, o, rows, :]
        if o == 1:
            inner = pl.ds(row_of(rho), Q)
            wh = lh[core, b, inner, :]
            wl = ll[core, b, inner, :]
        else:
            wh = rh[o // 2, rho, b]
            wl = rl[o // 2, rho, b]
        dot = functools.partial(jnp.dot, preferred_element_type=F32)
        out[o + b, rows, :] += dot(ah, wh) + dot(ah, wl) + dot(al, wh)

    def left_arrives(k):
        rho, b = BLOCKS[k]
        prow = par_row_of(rho)
        rows = pl.ds(prow, Q)
        keep_left(2 + core, b, prow, Q, par[b, rows, :])
        remote(par.at[b, rows], fwd.at[b, rows], fwd_send.at[k], fwd_recv.at[k], sibling).wait_recv()
        keep_left(3 - core, b, prow, Q, fwd[b, rows, :])

    def right_arrives(k):
        rho, b = BLOCKS[k]
        rows = pl.ds(row_of(rho), Q)
        for side, copy, panel in ((0, block_to_next, pre), (1, block_to_prev, fol)):
            copy(k, rho, b).wait_recv()
            hi, lo = split(panel[b, rows, :])
            if k < 11:
                rh[side, rho, b] = hi
                rl[side, rho, b] = lo
            else:
                last_h[side] = hi
                last_l[side] = lo

    def sibling_arrives(k):
        rho, b = BLOCKS[k]
        to_sibling(k, rho, b).wait_recv()
        r0 = row_of(rho)
        keep_left(1 - core, b, r0, Q, sib[b, pl.ds(r0, Q), :])

    first = pl.multiple_of((1 - half) * 2 * Q, 2 * Q)
    queue = []

    def add(when, cost, what, *args):
        queue.append((min(when, len(STEPS)), cost, functools.partial(what, *args)))

    def add_product(when, *args):
        add(when, args[-1], product, *args)

    for k in range(12):
        add(0, Q, sibling_arrives, k)
    for b in range(3):
        for rho in range(2):
            add_product(0, 1, b, rho, 0, 4 * Q)
    for k, (rho, b) in enumerate(BLOCKS):
        with_left = LAST[k] + LEFT_LAG
        with_right = LAST[k] + RIGHT_LAG
        crossed = LAST[k - 1] + RIGHT_LAG if k else 0
        rows = par_row_of(rho)
        add(with_left, 2 * Q, left_arrives, k)
        if b == 1:
            for c in range(3):
                for r in (2, 3):
                    add_product(with_left, 1, c, r, rows, Q)
        elif rho >= 2:
            for r in (2, 3):
                for c in range(3):
                    if 3 * r + c < k:
                        add_product(max(with_left, crossed), b, c, r, rows, Q)
        add(with_right, 2 * Q, right_arrives, k)
        for o in (0, 2) if k < 11 else ():
            if rho < 2 or 3 * rho + b >= 9 + o:
                add_product(with_right, o, b, rho, 0, 4 * Q)
            else:
                add_product(with_right, o, b, rho, first, 2 * Q)
                if 3 * rho + b >= 6 + o:
                    add_product(with_right, o, b, rho, par_row_of(2), Q)
    queue.sort(key=lambda entry: entry[0])

    for k, (rho, b) in enumerate(BLOCKS):
        load(k, rho, b).start()
    barrier = pltpu.get_barrier_semaphore()
    for device in (partner, sibling, nxt, prv):
        pl.semaphore_signal(barrier, inc=1, device_id=device, device_id_type=MESH)
    for k in range(2):
        load(k, *BLOCKS[k]).wait()
        mask_own(*BLOCKS[k])
    pl.semaphore_wait(barrier, 4)
    for k in range(2):
        send_block(k)
        to_sibling(k, *BLOCKS[k]).start()
    for k in range(2, 12):
        load(k, *BLOCKS[k]).wait()
        mask_own(*BLOCKS[k])
        to_sibling(k, *BLOCKS[k]).start()
    for j in range(5):
        out[j] = jnp.zeros_like(out[j])

    for s, step in enumerate(STEPS):
        k, _, _, i = step
        if i == 0 and k + 2 < 12:
            send_block(k + 2)
        forward(*step)
        spent = 0
        while queue and queue[0][0] <= s and spent < BUDGET:
            _, cost, what = queue.pop(0)
            what()
            spent += cost
    for _, _, what in queue:
        what()

    for k, (rho, b) in enumerate(BLOCKS):
        rows = pl.ds(row_of(rho), Q)
        prow = pl.ds(par_row_of(rho), Q)
        to_sibling(k, rho, b).wait_send()
        remote(own.at[b, rows], par.at[b, rows], par_send.at[k], par_recv.at[k, 0], partner).wait_send()
        remote(par.at[b, prow], fwd.at[b, prow], fwd_send.at[k], fwd_recv.at[k], sibling).wait_send()
        block_to_next(k, rho, b).wait_send()
        block_to_prev(k, rho, b).wait_send()


def finish(acc, lh, ll, last_h, last_l, out, done, sem):
    def write(src, j):
        return pltpu.make_async_copy(src, out.at[j], sem.at[j])

    for j in (0, 1, 3):
        write(acc.at[j], j).start()
    dot = functools.partial(jnp.dot, preferred_element_type=F32)
    for side, o in enumerate((0, 2)):
        ah, al, wh, wl = lh[3, o], ll[3, o], last_h[side], last_l[side]
        done[side] = acc[o + 2] + (dot(ah, wh) + dot(ah, wl) + dot(al, wh))
        write(done.at[side], o + 2).start()
    for j in range(5):
        write(acc.at[j], j).wait()


def local(density, tile_mask):
    dens = jnp.transpose(density, (1, 0, 2))
    mask = jnp.transpose(tile_mask, (1, 2, 0))
    panel = pltpu.VMEM(dens.shape, F32)
    dma = pltpu.SemaphoreType.DMA
    rows, cols = dens.shape[1:]
    left = pltpu.VMEM((4, 3, rows, cols), BF16)
    last = pltpu.VMEM((2, Q, cols), BF16)
    in_vmem = pl.BlockSpec(memory_space=pltpu.VMEM)
    held = pl.pallas_call(
        kernel,
        out_shape=(pltpu.VMEM((5, rows, cols), F32), left, left, last, last),
        in_specs=[pl.BlockSpec(memory_space=pl.ANY), pl.BlockSpec(memory_space=pltpu.SMEM)],
        out_specs=(in_vmem,) * 5,
        scratch_shapes=[panel] * 6
        + [pltpu.VMEM((2, 4, 3, Q, cols), BF16)] * 2
        + [dma((12,))] * 4
        + [dma((12, max(map(len, PIECES))))]
        + [dma((12,))] * 6,
        compiler_params=pltpu.CompilerParams(
            collective_id=0, has_side_effects=True, vmem_limit_bytes=40 * 1024 * 1024
        ),
    )(dens, mask)
    held = [pltpu.with_memory_space_constraint(x, pltpu.VMEM) for x in held]
    out = pl.pallas_call(
        finish,
        out_shape=jax.ShapeDtypeStruct((5, rows, cols), F32),
        in_specs=[in_vmem] * 5,
        out_specs=pl.BlockSpec(memory_space=pl.ANY),
        scratch_shapes=[pltpu.VMEM((2, rows, cols), F32), dma((5,))],
        compiler_params=pltpu.CompilerParams(vmem_limit_bytes=5 * 1024 * 1024),
    )(*held)
    return jnp.transpose(out, (1, 0, 2))


def solution(mesh):
    placed = (P("blk", None, "layer"), P("blk", None, "layer"))
    return jax.shard_map(
        local, mesh=mesh, in_specs=placed, out_specs=P("blk", None, "layer"), check_vma=False
    )
```

```python
import functools

import jax
import jax.numpy as jnp
from jax import lax
from jax.experimental import pallas as pl
from jax.experimental.pallas import tpu as pltpu
from jax.sharding import PartitionSpec as P

TILE = 128
Q = 256
PIECES = [[48, 48, 56, 56, 48]] * 11 + [[48, 56, 56, 48, 48]]
STEPS = [(k, sum(rows[:i]), n, i) for k, rows in enumerate(PIECES) for i, n in enumerate(rows)]
LAST = [max(s for s, step in enumerate(STEPS) if step[0] == k) for k in range(12)]
LATE = 96
LATE_AFTER, RELAY_AFTER, PASS_AFTER = 5, 7, 9
LEFT_LAG, RIGHT_LAG = 2, 9
BUDGET = 128 * 5
Y = 4
F32 = jnp.float32
BF16 = jnp.bfloat16
MESH = pl.DeviceIdType.MESH
BLOCKS = [(rho, b) for rho in range(4) for b in range(3)]


def kernel(
    dens, mask, out, lh, ll, last_h, last_l, own, sib, par, fwd, pre, fol, rh, rl, transit,
    load_sem, sib_send, sib_recv, par_send, par_recv, fwd_send, fwd_recv,
    nxt_send, pre_recv, prv_send, fol_recv, late_send, late_recv, relay_send, relay_recv, far_ok,
):
    blk = lax.axis_index("blk")
    lay = lax.axis_index("layer")
    nblk = lax.axis_size("blk")
    half = lay // 2
    core = lay % 2
    y = lax.rem(blk, Y)
    at_end = y == Y - 1
    at_start = y == 0
    other_half = (1 - half) * 2 + core
    partner = (blk, other_half)
    sibling = (blk, half * 2 + 1 - core)
    nxt = (lax.rem(blk + 1, nblk), jnp.where(at_end, other_half, lay))
    prv = (lax.rem(blk + nblk - 1, nblk), jnp.where(at_start, other_half, lay))

    beyond = (lax.rem(blk + jnp.where(y == 1, nblk - 3, 3), nblk), lay)

    def row_of(rho):
        return pl.multiple_of(lax.rem(2 * half + rho, 4) * Q, Q)

    def par_row_of(rho):
        return pl.multiple_of(lax.rem(2 * half + 2 + rho, 4) * Q, Q)

    def remote(src, dst, send, recv, to):
        return pltpu.make_async_remote_copy(
            src_ref=src, dst_ref=dst, send_sem=send, recv_sem=recv,
            device_id=to, device_id_type=MESH,
        )

    def load(k, rho, b):
        rows = pl.ds(row_of(rho), Q)
        return pltpu.make_async_copy(dens.at[b, rows], own.at[b, rows], load_sem.at[k])

    def to_sibling(k, rho, b):
        rows = pl.ds(row_of(rho), Q)
        return remote(own.at[b, rows], sib.at[b, rows], sib_send.at[k], sib_recv.at[k], sibling)

    def to_partner(k, offset, n, i):
        rho, b = BLOCKS[k]
        rows = pl.ds(row_of(rho) + offset, n)
        return remote(own.at[b, rows], par.at[b, rows], par_send.at[k], par_recv.at[k, i], partner)

    def panel_rows(k, rho):
        return pl.ds(row_of(rho), Q if k < 11 else Q - LATE)

    def block_to_next(k, rho, b):
        rows = panel_rows(k, rho)
        return remote(own.at[b, rows], pre.at[b, rows], nxt_send.at[k], pre_recv.at[k], nxt)

    def block_to_prev(k, rho, b):
        rows = panel_rows(k, rho)
        return remote(own.at[b, rows], fol.at[b, rows], prv_send.at[k], fol_recv.at[k], prv)

    late = (2, pl.ds(row_of(3) + Q - LATE, LATE))

    def late_to_next():
        return remote(own.at[late], pre.at[late], late_send.at[0], late_recv.at[0], nxt)

    def late_to_prev():
        return remote(own.at[late], fol.at[late], late_send.at[1], late_recv.at[1], prv)

    def late_across(panel):
        return remote(panel.at[late], transit, relay_send.at[0], relay_recv.at[0], beyond)

    def late_on(panel, recv, to):
        return remote(transit, panel.at[late], relay_send.at[1], recv, to)

    def send_late():
        @pl.when(jnp.logical_not(at_end))
        def _():
            late_to_next().start()

        @pl.when(jnp.logical_not(at_start))
        def _():
            late_to_prev().start()

    def relay_late():
        @pl.when(y == 2)
        def _():
            late_to_prev().wait_recv()
            late_across(fol).start()

        @pl.when(y == 1)
        def _():
            late_to_next().wait_recv()
            late_across(pre).start()

    def pass_late():
        @pl.when((y == 1) | (y == 2))
        def _():
            late_across(fol).wait_recv()

        @pl.when(y == 1)
        def _():
            late_on(pre, late_recv.at[0], prv).start()

        @pl.when(y == 2)
        def _():
            late_on(fol, late_recv.at[1], nxt).start()

    def late_arrives():
        @pl.when(y != 1)
        def _():
            late_to_next().wait_recv()

        @pl.when(y != 2)
        def _():
            late_to_prev().wait_recv()

    def late_sent():
        @pl.when(jnp.logical_not(at_end))
        def _():
            late_to_next().wait_send()

        @pl.when(jnp.logical_not(at_start))
        def _():
            late_to_prev().wait_send()

        @pl.when((y == 1) | (y == 2))
        def _():
            late_across(fol).wait_send()
            late_on(fol, late_recv.at[1], nxt).wait_send()

    def send_block(k):
        rho, b = BLOCKS[k]
        for step in STEPS:
            if step[0] == k:
                to_partner(*step).start()

        @pl.when(jnp.logical_not(at_end))
        def _():
            block_to_next(k, rho, b).start()

        @pl.when(jnp.logical_not(at_start))
        def _():
            block_to_prev(k, rho, b).start()

    def forward(k, offset, n, i):
        rho, b = BLOCKS[k]
        rows = pl.ds(par_row_of(rho) + offset, n)
        remote(own.at[b, rows], par.at[b, rows], par_send.at[k], par_recv.at[k, i], partner).wait_recv()
        remote(par.at[b, rows], fwd.at[b, rows], fwd_send.at[k], fwd_recv.at[k], sibling).start()

        if k == 11 and offset >= Q - LATE:
            return

        @pl.when(at_end)
        def _():
            remote(par.at[b, rows], pre.at[b, rows], nxt_send.at[k], pre_recv.at[k], nxt).start()

        @pl.when(at_start)
        def _():
            if k == 0 and i == 0:
                pl.semaphore_wait(far_ok, 1)
            remote(par.at[b, rows], fol.at[b, rows], prv_send.at[k], fol_recv.at[k], prv).start()

    def split(x):
        hi = x.astype(BF16)
        return hi, (x - hi.astype(F32)).astype(BF16)

    def keep_left(slot, o, r0, n, x):
        hi, lo = split(x)
        lh[slot, o, pl.ds(r0, n), :] = hi
        ll[slot, o, pl.ds(r0, n), :] = lo

    def mask_own(rho, b):
        r0 = row_of(rho)
        t0 = lax.rem(2 * half + rho, 4) * 2
        for t in range(2):
            for j in range(2):
                m = mask[b, j, t0 + t].astype(F32)
                rows = pl.ds(r0 + t * TILE, TILE)
                cols = pl.ds(j * TILE, TILE)
                x = own[b, rows, cols] * m
                own[b, rows, cols] = x
                hi, lo = split(x)
                lh[core, b, rows, cols] = hi
                ll[core, b, rows, cols] = lo

    def product(o, b, rho, r0, n):
        rows = pl.ds(r0, n)
        ah = lh[rho, o, rows, :]
        al = ll[rho, o, rows, :]
        if o == 1:
            inner = pl.ds(row_of(rho), Q)
            wh = lh[core, b, inner, :]
            wl = ll[core, b, inner, :]
        else:
            wh = rh[o // 2, rho, b]
            wl = rl[o // 2, rho, b]
        dot = functools.partial(jnp.dot, preferred_element_type=F32)
        out[o + b, rows, :] += dot(ah, wh) + dot(ah, wl) + dot(al, wh)

    def left_arrives(k):
        rho, b = BLOCKS[k]
        prow = par_row_of(rho)
        rows = pl.ds(prow, Q)
        keep_left(2 + core, b, prow, Q, par[b, rows, :])
        remote(par.at[b, rows], fwd.at[b, rows], fwd_send.at[k], fwd_recv.at[k], sibling).wait_recv()
        keep_left(3 - core, b, prow, Q, fwd[b, rows, :])

    def right_arrives(k):
        rho, b = BLOCKS[k]
        if k == 11:
            late_arrives()
        rows = pl.ds(row_of(rho), Q)
        for side, copy, panel in ((0, block_to_next, pre), (1, block_to_prev, fol)):
            copy(k, rho, b).wait_recv()
            hi, lo = split(panel[b, rows, :])
            if k < 11:
                rh[side, rho, b] = hi
                rl[side, rho, b] = lo
            else:
                last_h[side] = hi
                last_l[side] = lo

    def sibling_arrives(k):
        rho, b = BLOCKS[k]
        to_sibling(k, rho, b).wait_recv()
        r0 = row_of(rho)
        keep_left(1 - core, b, r0, Q, sib[b, pl.ds(r0, Q), :])

    first = pl.multiple_of((1 - half) * 2 * Q, 2 * Q)
    queue = []

    def add(when, cost, what, *args):
        queue.append((min(when, len(STEPS)), cost, functools.partial(what, *args)))

    def add_product(when, *args):
        add(when, args[-1], product, *args)

    for k in range(12):
        add(0, Q, sibling_arrives, k)
    for b in range(3):
        for rho in range(2):
            add_product(0, 1, b, rho, 0, 4 * Q)
    for k, (rho, b) in enumerate(BLOCKS):
        with_left = LAST[k] + LEFT_LAG
        with_right = LAST[k] + RIGHT_LAG
        crossed = LAST[k - 1] + RIGHT_LAG if k else 0
        rows = par_row_of(rho)
        add(with_left, 2 * Q, left_arrives, k)
        if b == 1:
            for c in range(3):
                for r in (2, 3):
                    add_product(with_left, 1, c, r, rows, Q)
        elif rho >= 2:
            for r in (2, 3):
                for c in range(3):
                    if 3 * r + c < k:
                        add_product(max(with_left, crossed), b, c, r, rows, Q)
        add(with_right, 2 * Q, right_arrives, k)
        for o in (0, 2) if k < 11 else ():
            if rho < 2 or 3 * rho + b >= 9 + o:
                add_product(with_right, o, b, rho, 0, 4 * Q)
            else:
                add_product(with_right, o, b, rho, first, 2 * Q)
                if 3 * rho + b >= 6 + o:
                    add_product(with_right, o, b, rho, par_row_of(2), Q)
    queue.sort(key=lambda entry: entry[0])

    for k, (rho, b) in enumerate(BLOCKS):
        load(k, rho, b).start()
    barrier = pltpu.get_barrier_semaphore()
    for device in (partner, sibling, prv):
        pl.semaphore_signal(barrier, inc=1, device_id=device, device_id_type=MESH)

    @pl.when(jnp.logical_not(at_end))
    def _():
        pl.semaphore_signal(barrier, inc=1, device_id=nxt, device_id_type=MESH)

    for k in range(2):
        load(k, *BLOCKS[k]).wait()
        mask_own(*BLOCKS[k])
    @pl.when(at_start)
    def _():
        pl.semaphore_wait(barrier, 3)

    @pl.when(jnp.logical_not(at_start))
    def _():
        pl.semaphore_wait(barrier, 4)

    @pl.when(at_end)
    def _():
        pl.semaphore_signal(far_ok, inc=1, device_id=nxt, device_id_type=MESH)

    for k in range(2):
        send_block(k)
        to_sibling(k, *BLOCKS[k]).start()
    for k in range(2, 12):
        load(k, *BLOCKS[k]).wait()
        mask_own(*BLOCKS[k])
        to_sibling(k, *BLOCKS[k]).start()
    for j in range(5):
        out[j] = jnp.zeros_like(out[j])

    for s, step in enumerate(STEPS):
        k, _, _, i = step
        if i == 0 and k + 2 < 12:
            send_block(k + 2)
        forward(*step)
        if s == LAST[LATE_AFTER]:
            send_late()
        if s == LAST[RELAY_AFTER]:
            relay_late()
        if s == LAST[PASS_AFTER]:
            pass_late()
        spent = 0
        while queue and queue[0][0] <= s and spent < BUDGET:
            _, cost, what = queue.pop(0)
            what()
            spent += cost
    for _, _, what in queue:
        what()

    late_sent()
    for k, (rho, b) in enumerate(BLOCKS):
        rows = pl.ds(row_of(rho), Q)
        prow = pl.ds(par_row_of(rho), Q)
        to_sibling(k, rho, b).wait_send()
        remote(own.at[b, rows], par.at[b, rows], par_send.at[k], par_recv.at[k, 0], partner).wait_send()
        remote(par.at[b, prow], fwd.at[b, prow], fwd_send.at[k], fwd_recv.at[k], sibling).wait_send()
        block_to_next(k, rho, b).wait_send()
        block_to_prev(k, rho, b).wait_send()


def finish(acc, lh, ll, last_h, last_l, out, done, sem):
    def write(src, j):
        return pltpu.make_async_copy(src, out.at[j], sem.at[j])

    for j in (0, 1, 3):
        write(acc.at[j], j).start()
    dot = functools.partial(jnp.dot, preferred_element_type=F32)
    for side, o in enumerate((0, 2)):
        ah, al, wh, wl = lh[3, o], ll[3, o], last_h[side], last_l[side]
        done[side] = acc[o + 2] + (dot(ah, wh) + dot(ah, wl) + dot(al, wh))
        write(done.at[side], o + 2).start()
    for j in range(5):
        write(acc.at[j], j).wait()


def local(density, tile_mask):
    dens = jnp.transpose(density, (1, 0, 2))
    mask = jnp.transpose(tile_mask, (1, 2, 0))
    panel = pltpu.VMEM(dens.shape, F32)
    dma = pltpu.SemaphoreType.DMA
    rows, cols = dens.shape[1:]
    left = pltpu.VMEM((4, 3, rows, cols), BF16)
    last = pltpu.VMEM((2, Q, cols), BF16)
    in_vmem = pl.BlockSpec(memory_space=pltpu.VMEM)
    held = pl.pallas_call(
        kernel,
        out_shape=(pltpu.VMEM((5, rows, cols), F32), left, left, last, last),
        in_specs=[pl.BlockSpec(memory_space=pl.ANY), pl.BlockSpec(memory_space=pltpu.SMEM)],
        out_specs=(in_vmem,) * 5,
        scratch_shapes=[panel] * 6
        + [pltpu.VMEM((2, 4, 3, Q, cols), BF16)] * 2
        + [pltpu.VMEM((LATE, cols), F32)]
        + [dma((12,))] * 4
        + [dma((12, max(map(len, PIECES))))]
        + [dma((12,))] * 6
        + [dma((2,))] * 3
        + [dma((1,)), pltpu.SemaphoreType.REGULAR],
        compiler_params=pltpu.CompilerParams(
            collective_id=0, has_side_effects=True, vmem_limit_bytes=40 * 1024 * 1024
        ),
    )(dens, mask)
    held = [pltpu.with_memory_space_constraint(x, pltpu.VMEM) for x in held]
    out = pl.pallas_call(
        finish,
        out_shape=jax.ShapeDtypeStruct((5, rows, cols), F32),
        in_specs=[in_vmem] * 5,
        out_specs=pl.BlockSpec(memory_space=pl.ANY),
        scratch_shapes=[pltpu.VMEM((2, rows, cols), F32), dma((5,))],
        compiler_params=pltpu.CompilerParams(vmem_limit_bytes=5 * 1024 * 1024),
    )(*held)
    return jnp.transpose(out, (1, 0, 2))


def solution(mesh):
    placed = (P("blk", None, "layer"), P("blk", None, "layer"))
    return jax.shard_map(
        local, mesh=mesh, in_specs=placed, out_specs=P("blk", None, "layer"), check_vma=False
    )
```

```python
import functools

import jax
import jax.numpy as jnp
from jax import lax
from jax.experimental import pallas as pl
from jax.experimental.pallas import tpu as pltpu
from jax.sharding import PartitionSpec as P

TILE = 128
Q = 256
PIECES = [[48, 48, 56, 56, 48]] * 11 + [[48, 48, 64, 64, 32]]
STEPS = [(k, sum(rows[:i]), n, i) for k, rows in enumerate(PIECES) for i, n in enumerate(rows)]
LAST = [max(s for s, step in enumerate(STEPS) if step[0] == k) for k in range(12)]
LATE = 160
LATE_AFTER, RELAY_AFTER, PASS_AFTER = 5, 7, 9
LEFT_LAG, RIGHT_LAG = 2, 9
BUDGET = 128 * 5
Y = 4
F32 = jnp.float32
BF16 = jnp.bfloat16
MESH = pl.DeviceIdType.MESH
BLOCKS = [(rho, b) for rho in range(4) for b in range(3)]


def kernel(
    dens, mask, out, lh, ll, last_h, last_l, own, sib, par, fwd, pre, fol, rh, rl, transit,
    load_sem, sib_send, sib_recv, par_send, par_recv, fwd_send, fwd_recv,
    nxt_send, pre_recv, prv_send, fol_recv, late_send, late_recv, relay_send, relay_recv, far_ok,
):
    blk = lax.axis_index("blk")
    lay = lax.axis_index("layer")
    nblk = lax.axis_size("blk")
    half = lay // 2
    core = lay % 2
    y = lax.rem(blk, Y)
    at_end = y == Y - 1
    at_start = y == 0
    other_half = (1 - half) * 2 + core
    partner = (blk, other_half)
    sibling = (blk, half * 2 + 1 - core)
    nxt = (lax.rem(blk + 1, nblk), jnp.where(at_end, other_half, lay))
    prv = (lax.rem(blk + nblk - 1, nblk), jnp.where(at_start, other_half, lay))

    beyond = (lax.rem(blk + jnp.where(y == 1, nblk - 3, 3), nblk), lay)

    def row_of(rho):
        return pl.multiple_of(lax.rem(2 * half + rho, 4) * Q, Q)

    def par_row_of(rho):
        return pl.multiple_of(lax.rem(2 * half + 2 + rho, 4) * Q, Q)

    def remote(src, dst, send, recv, to):
        return pltpu.make_async_remote_copy(
            src_ref=src, dst_ref=dst, send_sem=send, recv_sem=recv,
            device_id=to, device_id_type=MESH,
        )

    def load(k, rho, b):
        rows = pl.ds(row_of(rho), Q)
        return pltpu.make_async_copy(dens.at[b, rows], own.at[b, rows], load_sem.at[k])

    def to_sibling(k, rho, b):
        rows = pl.ds(row_of(rho), Q)
        return remote(own.at[b, rows], sib.at[b, rows], sib_send.at[k], sib_recv.at[k], sibling)

    def to_partner(k, offset, n, i):
        rho, b = BLOCKS[k]
        rows = pl.ds(row_of(rho) + offset, n)
        return remote(own.at[b, rows], par.at[b, rows], par_send.at[k], par_recv.at[k, i], partner)

    def panel_rows(k, rho):
        return pl.ds(row_of(rho), Q if k < 11 else Q - LATE)

    def block_to_next(k, rho, b):
        rows = panel_rows(k, rho)
        return remote(own.at[b, rows], pre.at[b, rows], nxt_send.at[k], pre_recv.at[k], nxt)

    def block_to_prev(k, rho, b):
        rows = panel_rows(k, rho)
        return remote(own.at[b, rows], fol.at[b, rows], prv_send.at[k], fol_recv.at[k], prv)

    late = (2, pl.ds(row_of(3) + Q - LATE, LATE))

    def late_to_next():
        return remote(own.at[late], pre.at[late], late_send.at[0], late_recv.at[0], nxt)

    def late_to_prev():
        return remote(own.at[late], fol.at[late], late_send.at[1], late_recv.at[1], prv)

    def late_across(panel):
        return remote(panel.at[late], transit, relay_send.at[0], relay_recv.at[0], beyond)

    def late_on(panel, recv, to):
        return remote(transit, panel.at[late], relay_send.at[1], recv, to)

    def send_late():
        @pl.when(jnp.logical_not(at_end))
        def _():
            late_to_next().start()

        @pl.when(jnp.logical_not(at_start))
        def _():
            late_to_prev().start()

    def relay_late():
        @pl.when(y == 2)
        def _():
            late_to_prev().wait_recv()
            late_across(fol).start()

        @pl.when(y == 1)
        def _():
            late_to_next().wait_recv()
            late_across(pre).start()

    def pass_late():
        @pl.when((y == 1) | (y == 2))
        def _():
            late_across(fol).wait_recv()

        @pl.when(y == 1)
        def _():
            late_on(pre, late_recv.at[0], prv).start()

        @pl.when(y == 2)
        def _():
            late_on(fol, late_recv.at[1], nxt).start()

    def late_arrives():
        @pl.when(y != 1)
        def _():
            late_to_next().wait_recv()

        @pl.when(y != 2)
        def _():
            late_to_prev().wait_recv()

    def late_sent():
        @pl.when(jnp.logical_not(at_end))
        def _():
            late_to_next().wait_send()

        @pl.when(jnp.logical_not(at_start))
        def _():
            late_to_prev().wait_send()

        @pl.when((y == 1) | (y == 2))
        def _():
            late_across(fol).wait_send()
            late_on(fol, late_recv.at[1], nxt).wait_send()

    def send_block(k):
        rho, b = BLOCKS[k]
        for step in STEPS:
            if step[0] == k:
                to_partner(*step).start()

        @pl.when(jnp.logical_not(at_end))
        def _():
            block_to_next(k, rho, b).start()

        @pl.when(jnp.logical_not(at_start))
        def _():
            block_to_prev(k, rho, b).start()

    def forward(k, offset, n, i):
        rho, b = BLOCKS[k]
        rows = pl.ds(par_row_of(rho) + offset, n)
        remote(own.at[b, rows], par.at[b, rows], par_send.at[k], par_recv.at[k, i], partner).wait_recv()
        remote(par.at[b, rows], fwd.at[b, rows], fwd_send.at[k], fwd_recv.at[k], sibling).start()

        if k == 11 and offset >= Q - LATE:
            return

        @pl.when(at_end)
        def _():
            remote(par.at[b, rows], pre.at[b, rows], nxt_send.at[k], pre_recv.at[k], nxt).start()

        @pl.when(at_start)
        def _():
            if k == 0 and i == 0:
                pl.semaphore_wait(far_ok, 1)
            remote(par.at[b, rows], fol.at[b, rows], prv_send.at[k], fol_recv.at[k], prv).start()

    def split(x):
        hi = x.astype(BF16)
        return hi, (x - hi.astype(F32)).astype(BF16)

    def keep_left(slot, o, r0, n, x):
        hi, lo = split(x)
        lh[slot, o, pl.ds(r0, n), :] = hi
        ll[slot, o, pl.ds(r0, n), :] = lo

    def mask_own(rho, b):
        r0 = row_of(rho)
        t0 = lax.rem(2 * half + rho, 4) * 2
        for t in range(2):
            for j in range(2):
                m = mask[b, j, t0 + t].astype(F32)
                rows = pl.ds(r0 + t * TILE, TILE)
                cols = pl.ds(j * TILE, TILE)
                x = own[b, rows, cols] * m
                own[b, rows, cols] = x
                hi, lo = split(x)
                lh[core, b, rows, cols] = hi
                ll[core, b, rows, cols] = lo

    def product(o, b, rho, r0, n):
        rows = pl.ds(r0, n)
        ah = lh[rho, o, rows, :]
        al = ll[rho, o, rows, :]
        if o == 1:
            inner = pl.ds(row_of(rho), Q)
            wh = lh[core, b, inner, :]
            wl = ll[core, b, inner, :]
        else:
            wh = rh[o // 2, rho, b]
            wl = rl[o // 2, rho, b]
        dot = functools.partial(jnp.dot, preferred_element_type=F32)
        out[o + b, rows, :] += dot(ah, wh) + dot(ah, wl) + dot(al, wh)

    def left_arrives(k):
        rho, b = BLOCKS[k]
        prow = par_row_of(rho)
        rows = pl.ds(prow, Q)
        keep_left(2 + core, b, prow, Q, par[b, rows, :])
        remote(par.at[b, rows], fwd.at[b, rows], fwd_send.at[k], fwd_recv.at[k], sibling).wait_recv()
        keep_left(3 - core, b, prow, Q, fwd[b, rows, :])

    def right_arrives(k):
        rho, b = BLOCKS[k]
        if k == 11:
            late_arrives()
        rows = pl.ds(row_of(rho), Q)
        for side, copy, panel in ((0, block_to_next, pre), (1, block_to_prev, fol)):
            copy(k, rho, b).wait_recv()
            hi, lo = split(panel[b, rows, :])
            if k < 11:
                rh[side, rho, b] = hi
                rl[side, rho, b] = lo
            else:
                last_h[side] = hi
                last_l[side] = lo

    def sibling_arrives(k):
        rho, b = BLOCKS[k]
        to_sibling(k, rho, b).wait_recv()
        r0 = row_of(rho)
        keep_left(1 - core, b, r0, Q, sib[b, pl.ds(r0, Q), :])

    first = pl.multiple_of((1 - half) * 2 * Q, 2 * Q)
    queue = []

    def add(when, cost, what, *args):
        queue.append((min(when, len(STEPS)), cost, functools.partial(what, *args)))

    def add_product(when, *args):
        add(when, args[-1], product, *args)

    for k in range(12):
        add(0, Q, sibling_arrives, k)
    for b in range(3):
        for rho in range(2):
            add_product(0, 1, b, rho, 0, 4 * Q)
    for k, (rho, b) in enumerate(BLOCKS):
        with_left = LAST[k] + LEFT_LAG
        with_right = LAST[k] + RIGHT_LAG
        crossed = LAST[k - 1] + RIGHT_LAG if k else 0
        rows = par_row_of(rho)
        add(with_left, 2 * Q, left_arrives, k)
        if b == 1:
            for c in range(3):
                for r in (2, 3):
                    add_product(with_left, 1, c, r, rows, Q)
        elif rho >= 2:
            for r in (2, 3):
                for c in range(3):
                    if 3 * r + c < k:
                        add_product(max(with_left, crossed), b, c, r, rows, Q)
        add(with_right, 2 * Q, right_arrives, k)
        for o in (0, 2) if k < 11 else ():
            if rho < 2 or 3 * rho + b >= 9 + o:
                add_product(with_right, o, b, rho, 0, 4 * Q)
            else:
                add_product(with_right, o, b, rho, first, 2 * Q)
                if 3 * rho + b >= 6 + o:
                    add_product(with_right, o, b, rho, par_row_of(2), Q)
    queue.sort(key=lambda entry: entry[0])

    for k, (rho, b) in enumerate(BLOCKS):
        load(k, rho, b).start()
    barrier = pltpu.get_barrier_semaphore()
    for device in (partner, sibling, prv):
        pl.semaphore_signal(barrier, inc=1, device_id=device, device_id_type=MESH)

    @pl.when(jnp.logical_not(at_end))
    def _():
        pl.semaphore_signal(barrier, inc=1, device_id=nxt, device_id_type=MESH)

    for k in range(2):
        load(k, *BLOCKS[k]).wait()
        mask_own(*BLOCKS[k])
    @pl.when(at_start)
    def _():
        pl.semaphore_wait(barrier, 3)

    @pl.when(jnp.logical_not(at_start))
    def _():
        pl.semaphore_wait(barrier, 4)

    @pl.when(at_end)
    def _():
        pl.semaphore_signal(far_ok, inc=1, device_id=nxt, device_id_type=MESH)

    for k in range(2):
        send_block(k)
        to_sibling(k, *BLOCKS[k]).start()
    for k in range(2, 12):
        load(k, *BLOCKS[k]).wait()
        mask_own(*BLOCKS[k])
        to_sibling(k, *BLOCKS[k]).start()
    for j in range(5):
        out[j] = jnp.zeros_like(out[j])

    for s, step in enumerate(STEPS):
        k, _, _, i = step
        if i == 0 and k + 2 < 12:
            send_block(k + 2)
        forward(*step)
        if s == LAST[LATE_AFTER]:
            send_late()
        if s == LAST[RELAY_AFTER]:
            relay_late()
        if s == LAST[PASS_AFTER]:
            pass_late()
        spent = 0
        while queue and queue[0][0] <= s and spent < BUDGET:
            _, cost, what = queue.pop(0)
            what()
            spent += cost
    for _, _, what in queue:
        what()

    late_sent()
    for k, (rho, b) in enumerate(BLOCKS):
        rows = pl.ds(row_of(rho), Q)
        prow = pl.ds(par_row_of(rho), Q)
        to_sibling(k, rho, b).wait_send()
        remote(own.at[b, rows], par.at[b, rows], par_send.at[k], par_recv.at[k, 0], partner).wait_send()
        remote(par.at[b, prow], fwd.at[b, prow], fwd_send.at[k], fwd_recv.at[k], sibling).wait_send()
        block_to_next(k, rho, b).wait_send()
        block_to_prev(k, rho, b).wait_send()


def finish(acc, lh, ll, last_h, last_l, out, done, sem):
    def write(src, j):
        return pltpu.make_async_copy(src, out.at[j], sem.at[j])

    for j in (0, 1, 3):
        write(acc.at[j], j).start()
    dot = functools.partial(jnp.dot, preferred_element_type=F32)
    for side, o in enumerate((0, 2)):
        ah, al, wh, wl = lh[3, o], ll[3, o], last_h[side], last_l[side]
        done[side] = acc[o + 2] + (dot(ah, wh) + dot(ah, wl) + dot(al, wh))
        write(done.at[side], o + 2).start()
    for j in range(5):
        write(acc.at[j], j).wait()


def local(density, tile_mask):
    dens = jnp.transpose(density, (1, 0, 2))
    mask = jnp.transpose(tile_mask, (1, 2, 0))
    panel = pltpu.VMEM(dens.shape, F32)
    dma = pltpu.SemaphoreType.DMA
    rows, cols = dens.shape[1:]
    left = pltpu.VMEM((4, 3, rows, cols), BF16)
    last = pltpu.VMEM((2, Q, cols), BF16)
    in_vmem = pl.BlockSpec(memory_space=pltpu.VMEM)
    held = pl.pallas_call(
        kernel,
        out_shape=(pltpu.VMEM((5, rows, cols), F32), left, left, last, last),
        in_specs=[pl.BlockSpec(memory_space=pl.ANY), pl.BlockSpec(memory_space=pltpu.SMEM)],
        out_specs=(in_vmem,) * 5,
        scratch_shapes=[panel] * 6
        + [pltpu.VMEM((2, 4, 3, Q, cols), BF16)] * 2
        + [pltpu.VMEM((LATE, cols), F32)]
        + [dma((12,))] * 4
        + [dma((12, max(map(len, PIECES))))]
        + [dma((12,))] * 6
        + [dma((2,))] * 3
        + [dma((1,)), pltpu.SemaphoreType.REGULAR],
        compiler_params=pltpu.CompilerParams(
            collective_id=0, has_side_effects=True, vmem_limit_bytes=40 * 1024 * 1024
        ),
    )(dens, mask)
    held = [pltpu.with_memory_space_constraint(x, pltpu.VMEM) for x in held]
    out = pl.pallas_call(
        finish,
        out_shape=jax.ShapeDtypeStruct((5, rows, cols), F32),
        in_specs=[in_vmem] * 5,
        out_specs=pl.BlockSpec(memory_space=pl.ANY),
        scratch_shapes=[pltpu.VMEM((2, rows, cols), F32), dma((5,))],
        compiler_params=pltpu.CompilerParams(vmem_limit_bytes=5 * 1024 * 1024),
    )(*held)
    return jnp.transpose(out, (1, 0, 2))


def solution(mesh):
    placed = (P("blk", None, "layer"), P("blk", None, "layer"))
    return jax.shard_map(
        local, mesh=mesh, in_specs=placed, out_specs=P("blk", None, "layer"), check_vma=False
    )
```

```python
import functools

import jax
import jax.numpy as jnp
from jax import lax
from jax.experimental import pallas as pl
from jax.experimental.pallas import tpu as pltpu
from jax.sharding import PartitionSpec as P

TILE = 128
Q = 256
PIECES = [[48, 48, 56, 56, 48]] * 11 + [[32, 32, 32, 64, 96]]
STEPS = [(k, sum(rows[:i]), n, i) for k, rows in enumerate(PIECES) for i, n in enumerate(rows)]
LAST = [max(s for s, step in enumerate(STEPS) if step[0] == k) for k in range(12)]
LATE = 160
LATE_AFTER, RELAY_AFTER, PASS_AFTER = 5, 7, 9
LEFT_LAG, RIGHT_LAG = 2, 9
BUDGET = 128 * 5
Y = 4
F32 = jnp.float32
BF16 = jnp.bfloat16
MESH = pl.DeviceIdType.MESH
BLOCKS = [(rho, b) for rho in range(4) for b in range(3)]


def kernel(
    dens, mask, out, lh, ll, last_h, last_l, own, sib, par, fwd, pre, fol, rh, rl, transit,
    load_sem, sib_send, sib_recv, par_send, par_recv, fwd_send, fwd_recv,
    nxt_send, pre_recv, prv_send, fol_recv, late_send, late_recv, relay_send, relay_recv, far_ok,
):
    blk = lax.axis_index("blk")
    lay = lax.axis_index("layer")
    nblk = lax.axis_size("blk")
    half = lay // 2
    core = lay % 2
    y = lax.rem(blk, Y)
    at_end = y == Y - 1
    at_start = y == 0
    other_half = (1 - half) * 2 + core
    partner = (blk, other_half)
    sibling = (blk, half * 2 + 1 - core)
    nxt = (lax.rem(blk + 1, nblk), jnp.where(at_end, other_half, lay))
    prv = (lax.rem(blk + nblk - 1, nblk), jnp.where(at_start, other_half, lay))

    beyond = (lax.rem(blk + jnp.where(y == 1, nblk - 3, 3), nblk), lay)

    def row_of(rho):
        return pl.multiple_of(lax.rem(2 * half + rho, 4) * Q, Q)

    def par_row_of(rho):
        return pl.multiple_of(lax.rem(2 * half + 2 + rho, 4) * Q, Q)

    def remote(src, dst, send, recv, to):
        return pltpu.make_async_remote_copy(
            src_ref=src, dst_ref=dst, send_sem=send, recv_sem=recv,
            device_id=to, device_id_type=MESH,
        )

    def load(k, rho, b):
        rows = pl.ds(row_of(rho), Q)
        return pltpu.make_async_copy(dens.at[b, rows], own.at[b, rows], load_sem.at[k])

    def to_sibling(k, rho, b):
        rows = pl.ds(row_of(rho), Q)
        return remote(own.at[b, rows], sib.at[b, rows], sib_send.at[k], sib_recv.at[k], sibling)

    def to_partner(k, offset, n, i):
        rho, b = BLOCKS[k]
        rows = pl.ds(row_of(rho) + offset, n)
        return remote(own.at[b, rows], par.at[b, rows], par_send.at[k], par_recv.at[k, i], partner)

    def panel_rows(k, rho):
        return pl.ds(row_of(rho), Q if k < 11 else Q - LATE)

    def block_to_next(k, rho, b):
        rows = panel_rows(k, rho)
        return remote(own.at[b, rows], pre.at[b, rows], nxt_send.at[k], pre_recv.at[k], nxt)

    def block_to_prev(k, rho, b):
        rows = panel_rows(k, rho)
        return remote(own.at[b, rows], fol.at[b, rows], prv_send.at[k], fol_recv.at[k], prv)

    late = (2, pl.ds(row_of(3) + Q - LATE, LATE))

    def late_to_next():
        return remote(own.at[late], pre.at[late], late_send.at[0], late_recv.at[0], nxt)

    def late_to_prev():
        return remote(own.at[late], fol.at[late], late_send.at[1], late_recv.at[1], prv)

    def late_across(panel):
        return remote(panel.at[late], transit, relay_send.at[0], relay_recv.at[0], beyond)

    def late_on(panel, recv, to):
        return remote(transit, panel.at[late], relay_send.at[1], recv, to)

    def send_late():
        @pl.when(jnp.logical_not(at_end))
        def _():
            late_to_next().start()

        @pl.when(jnp.logical_not(at_start))
        def _():
            late_to_prev().start()

    def relay_late():
        @pl.when(y == 2)
        def _():
            late_to_prev().wait_recv()
            late_across(fol).start()

        @pl.when(y == 1)
        def _():
            late_to_next().wait_recv()
            late_across(pre).start()

    def pass_late():
        @pl.when((y == 1) | (y == 2))
        def _():
            late_across(fol).wait_recv()

        @pl.when(y == 1)
        def _():
            late_on(pre, late_recv.at[0], prv).start()

        @pl.when(y == 2)
        def _():
            late_on(fol, late_recv.at[1], nxt).start()

    def late_arrives():
        @pl.when(y != 1)
        def _():
            late_to_next().wait_recv()

        @pl.when(y != 2)
        def _():
            late_to_prev().wait_recv()

    def late_sent():
        @pl.when(jnp.logical_not(at_end))
        def _():
            late_to_next().wait_send()

        @pl.when(jnp.logical_not(at_start))
        def _():
            late_to_prev().wait_send()

        @pl.when((y == 1) | (y == 2))
        def _():
            late_across(fol).wait_send()
            late_on(fol, late_recv.at[1], nxt).wait_send()

    def send_block(k):
        rho, b = BLOCKS[k]
        for step in STEPS:
            if step[0] == k:
                to_partner(*step).start()

        @pl.when(jnp.logical_not(at_end))
        def _():
            block_to_next(k, rho, b).start()

        @pl.when(jnp.logical_not(at_start))
        def _():
            block_to_prev(k, rho, b).start()

    def forward(k, offset, n, i):
        rho, b = BLOCKS[k]
        rows = pl.ds(par_row_of(rho) + offset, n)
        remote(own.at[b, rows], par.at[b, rows], par_send.at[k], par_recv.at[k, i], partner).wait_recv()
        remote(par.at[b, rows], fwd.at[b, rows], fwd_send.at[k], fwd_recv.at[k], sibling).start()

        if k == 11 and offset >= Q - LATE:
            return

        @pl.when(at_end)
        def _():
            remote(par.at[b, rows], pre.at[b, rows], nxt_send.at[k], pre_recv.at[k], nxt).start()

        @pl.when(at_start)
        def _():
            if k == 0 and i == 0:
                pl.semaphore_wait(far_ok, 1)
            remote(par.at[b, rows], fol.at[b, rows], prv_send.at[k], fol_recv.at[k], prv).start()

    def split(x):
        hi = x.astype(BF16)
        return hi, (x - hi.astype(F32)).astype(BF16)

    def keep_left(slot, o, r0, n, x):
        hi, lo = split(x)
        lh[slot, o, pl.ds(r0, n), :] = hi
        ll[slot, o, pl.ds(r0, n), :] = lo

    def mask_own(rho, b):
        r0 = row_of(rho)
        t0 = lax.rem(2 * half + rho, 4) * 2
        for t in range(2):
            for j in range(2):
                m = mask[b, j, t0 + t].astype(F32)
                rows = pl.ds(r0 + t * TILE, TILE)
                cols = pl.ds(j * TILE, TILE)
                x = own[b, rows, cols] * m
                own[b, rows, cols] = x
                hi, lo = split(x)
                lh[core, b, rows, cols] = hi
                ll[core, b, rows, cols] = lo

    def product(o, b, rho, r0, n):
        rows = pl.ds(r0, n)
        ah = lh[rho, o, rows, :]
        al = ll[rho, o, rows, :]
        if o == 1:
            inner = pl.ds(row_of(rho), Q)
            wh = lh[core, b, inner, :]
            wl = ll[core, b, inner, :]
        else:
            wh = rh[o // 2, rho, b]
            wl = rl[o // 2, rho, b]
        dot = functools.partial(jnp.dot, preferred_element_type=F32)
        out[o + b, rows, :] += dot(ah, wh) + dot(ah, wl) + dot(al, wh)

    def left_arrives(k):
        rho, b = BLOCKS[k]
        prow = par_row_of(rho)
        rows = pl.ds(prow, Q)
        keep_left(2 + core, b, prow, Q, par[b, rows, :])
        remote(par.at[b, rows], fwd.at[b, rows], fwd_send.at[k], fwd_recv.at[k], sibling).wait_recv()
        keep_left(3 - core, b, prow, Q, fwd[b, rows, :])

    def right_arrives(k):
        rho, b = BLOCKS[k]
        if k == 11:
            late_arrives()
        rows = pl.ds(row_of(rho), Q)
        for side, copy, panel in ((0, block_to_next, pre), (1, block_to_prev, fol)):
            copy(k, rho, b).wait_recv()
            hi, lo = split(panel[b, rows, :])
            if k < 11:
                rh[side, rho, b] = hi
                rl[side, rho, b] = lo
            else:
                last_h[side] = hi
                last_l[side] = lo

    def sibling_arrives(k):
        rho, b = BLOCKS[k]
        to_sibling(k, rho, b).wait_recv()
        r0 = row_of(rho)
        keep_left(1 - core, b, r0, Q, sib[b, pl.ds(r0, Q), :])

    first = pl.multiple_of((1 - half) * 2 * Q, 2 * Q)
    queue = []

    def add(when, cost, what, *args):
        queue.append((min(when, len(STEPS)), cost, functools.partial(what, *args)))

    def add_product(when, *args):
        add(when, args[-1], product, *args)

    for k in range(12):
        add(0, Q, sibling_arrives, k)
    for b in range(3):
        for rho in range(2):
            add_product(0, 1, b, rho, 0, 4 * Q)
    for k, (rho, b) in enumerate(BLOCKS):
        with_left = LAST[k] + LEFT_LAG
        with_right = LAST[k] + RIGHT_LAG
        crossed = LAST[k - 1] + RIGHT_LAG if k else 0
        rows = par_row_of(rho)
        add(with_left, 2 * Q, left_arrives, k)
        if b == 1:
            for c in range(3):
                for r in (2, 3):
                    add_product(with_left, 1, c, r, rows, Q)
        elif rho >= 2:
            for r in (2, 3):
                for c in range(3):
                    if 3 * r + c < k:
                        add_product(max(with_left, crossed), b, c, r, rows, Q)
        add(with_right, 2 * Q, right_arrives, k)
        for o in (0, 2) if k < 11 else ():
            if rho < 2 or 3 * rho + b >= 9 + o:
                add_product(with_right, o, b, rho, 0, 4 * Q)
            else:
                add_product(with_right, o, b, rho, first, 2 * Q)
                if 3 * rho + b >= 6 + o:
                    add_product(with_right, o, b, rho, par_row_of(2), Q)
    queue.sort(key=lambda entry: entry[0])

    for k, (rho, b) in enumerate(BLOCKS):
        load(k, rho, b).start()
    barrier = pltpu.get_barrier_semaphore()
    for device in (partner, sibling, prv):
        pl.semaphore_signal(barrier, inc=1, device_id=device, device_id_type=MESH)

    @pl.when(jnp.logical_not(at_end))
    def _():
        pl.semaphore_signal(barrier, inc=1, device_id=nxt, device_id_type=MESH)

    for k in range(2):
        load(k, *BLOCKS[k]).wait()
        mask_own(*BLOCKS[k])
    @pl.when(at_start)
    def _():
        pl.semaphore_wait(barrier, 3)

    @pl.when(jnp.logical_not(at_start))
    def _():
        pl.semaphore_wait(barrier, 4)

    @pl.when(at_end)
    def _():
        pl.semaphore_signal(far_ok, inc=1, device_id=nxt, device_id_type=MESH)

    for k in range(2):
        send_block(k)
        to_sibling(k, *BLOCKS[k]).start()
    for k in range(2, 12):
        load(k, *BLOCKS[k]).wait()
        mask_own(*BLOCKS[k])
        to_sibling(k, *BLOCKS[k]).start()
    for j in range(5):
        out[j] = jnp.zeros_like(out[j])

    for s, step in enumerate(STEPS):
        k, _, _, i = step
        if i == 0 and k + 2 < 12:
            send_block(k + 2)
        forward(*step)
        if s == LAST[LATE_AFTER]:
            send_late()
        if s == LAST[RELAY_AFTER]:
            relay_late()
        if s == LAST[PASS_AFTER]:
            pass_late()
        spent = 0
        while queue and queue[0][0] <= s and spent < BUDGET:
            _, cost, what = queue.pop(0)
            what()
            spent += cost
    for _, _, what in queue:
        what()

    late_sent()
    for k, (rho, b) in enumerate(BLOCKS):
        rows = pl.ds(row_of(rho), Q)
        prow = pl.ds(par_row_of(rho), Q)
        to_sibling(k, rho, b).wait_send()
        remote(own.at[b, rows], par.at[b, rows], par_send.at[k], par_recv.at[k, 0], partner).wait_send()
        remote(par.at[b, prow], fwd.at[b, prow], fwd_send.at[k], fwd_recv.at[k], sibling).wait_send()
        block_to_next(k, rho, b).wait_send()
        block_to_prev(k, rho, b).wait_send()


def finish(acc, lh, ll, last_h, last_l, out, done, sem):
    def write(src, j):
        return pltpu.make_async_copy(src, out.at[j], sem.at[j])

    for j in (0, 1, 3):
        write(acc.at[j], j).start()
    dot = functools.partial(jnp.dot, preferred_element_type=F32)
    for side, o in enumerate((0, 2)):
        ah, al, wh, wl = lh[3, o], ll[3, o], last_h[side], last_l[side]
        done[side] = acc[o + 2] + (dot(ah, wh) + dot(ah, wl) + dot(al, wh))
        write(done.at[side], o + 2).start()
    for j in range(5):
        write(acc.at[j], j).wait()


def local(density, tile_mask):
    dens = jnp.transpose(density, (1, 0, 2))
    mask = jnp.transpose(tile_mask, (1, 2, 0))
    panel = pltpu.VMEM(dens.shape, F32)
    dma = pltpu.SemaphoreType.DMA
    rows, cols = dens.shape[1:]
    left = pltpu.VMEM((4, 3, rows, cols), BF16)
    last = pltpu.VMEM((2, Q, cols), BF16)
    in_vmem = pl.BlockSpec(memory_space=pltpu.VMEM)
    held = pl.pallas_call(
        kernel,
        out_shape=(pltpu.VMEM((5, rows, cols), F32), left, left, last, last),
        in_specs=[pl.BlockSpec(memory_space=pl.ANY), pl.BlockSpec(memory_space=pltpu.SMEM)],
        out_specs=(in_vmem,) * 5,
        scratch_shapes=[panel] * 6
        + [pltpu.VMEM((2, 4, 3, Q, cols), BF16)] * 2
        + [pltpu.VMEM((LATE, cols), F32)]
        + [dma((12,))] * 4
        + [dma((12, max(map(len, PIECES))))]
        + [dma((12,))] * 6
        + [dma((2,))] * 3
        + [dma((1,)), pltpu.SemaphoreType.REGULAR],
        compiler_params=pltpu.CompilerParams(
            collective_id=0, has_side_effects=True, vmem_limit_bytes=40 * 1024 * 1024
        ),
    )(dens, mask)
    held = [pltpu.with_memory_space_constraint(x, pltpu.VMEM) for x in held]
    out = pl.pallas_call(
        finish,
        out_shape=jax.ShapeDtypeStruct((5, rows, cols), F32),
        in_specs=[in_vmem] * 5,
        out_specs=pl.BlockSpec(memory_space=pl.ANY),
        scratch_shapes=[pltpu.VMEM((2, rows, cols), F32), dma((5,))],
        compiler_params=pltpu.CompilerParams(vmem_limit_bytes=5 * 1024 * 1024),
    )(*held)
    return jnp.transpose(out, (1, 0, 2))


def solution(mesh):
    placed = (P("blk", None, "layer"), P("blk", None, "layer"))
    return jax.shard_map(
        local, mesh=mesh, in_specs=placed, out_specs=P("blk", None, "layer"), check_vma=False
    )
```
